32 devices in a mesh: groups: 1, orient: 8 (over z, core), cls: 4 (over y, x).
Axes of the slice: x: 2, y: 2, z: 4, core: 2. Of those that a mesh axis runs over, the one named last changes fastest.
Arguments:
- particles: bfloat16 [384, 33024], P(('groups', 'orient', 'cls')), may hold values from -300 to 300
- projections: bfloat16 [8, 8, 33024], P('cls', 'orient')
- ctf: bfloat16 [8, 16512], replicated, may hold values from -1 to 1
- defocus_group: int32 [384], P(('groups', 'orient', 'cls')), may hold values from 0 to 7
- offsets: int32 [384, 2], P(('groups', 'orient', 'cls')), may hold values from -8 to 8
- routes: int32 [384, 4], P(('groups', 'orient', 'cls')), may hold values from 0 to 7, all different within a row; in each aligned block of 12 rows (0 to 11, 12 to 23, ...) at most 6 rows name the same one
Outputs:
- log_evidence: float32 [384], P(('groups', 'orient', 'cls'))
- data_sum: bfloat16 [8, 8, 33024], P(('groups', 'cls'), 'orient')
The draws below stay inside these ranges and needn't reach their ends.
Inputs may be any that keep to these rules, and one draw needn't show every extreme that they name: `routes`: the 4 blocks of a particle differ; among the particles of one device no block is listed more than 6 times, and some block is listed exactly 6 times.
All inputs are finite; a program needn't handle non-finite values.
Results may differ from the reference program's by a relative error of at most 0.01.
The reference program's roundings to bfloat16 on the way count: a program that leaves them out, or rounds other values in their place, can miss the bound.
Values may be sent and summed in bfloat16 or wider, within the bound.
A program may use at most 64 MiB of HBM per device.

```python
import math
import jax
import jax.numpy as jnp
import numpy as np
from jax import lax

KX = 86
KY = 192
BOX = 256
PIX = 16512
NDEF = 8
TOPK = 4
CLASSES = 8
ORI_DEV = 1
DIRECTIONS = 8
PART_DEV = 12
PARTICLES = 384
CAP = 6
N_ORIENT = 8
N_CLS = 4


def draw_particles(key, part):
    first_key = jax.random.fold_in(key, 0)
    shape = (PARTICLES, 2 * PIX)
    values = jnp.clip(jax.random.normal(first_key, shape, jnp.float32), -6.0, 6.0)
    return values.astype(jnp.bfloat16)


def draw_projections(key, part):
    first_key, second_key = jax.random.split(key)
    shape = (CLASSES, DIRECTIONS, 2 * PIX)
    values = jnp.clip(jax.random.normal(first_key, shape, jnp.float32), -6.0, 6.0)
    amplitude = jnp.exp(jax.random.uniform(second_key, (CLASSES, DIRECTIONS, 1), jnp.float32, 0.0, math.log(3.0)))
    return (values * amplitude * (1.0 / math.sqrt(2.0 * PIX))).astype(jnp.bfloat16)


def set_ends(drawn, rng, low, high):
    place = [jax.random.randint(jax.random.fold_in(rng, axis), (), 0, length) for axis, length in enumerate(drawn.shape)]
    widest = drawn.shape.index(max(drawn.shape))
    next_to = place[:widest] + [(place[widest] + 1) % drawn.shape[widest]] + place[widest + 1:]
    return drawn.at[tuple(place)].set(low).at[tuple(next_to)].set(high)


def deal_out(stream_key, own, number, rows, number_of, top, bound, slope):
    ranking = jax.random.permutation(stream_key, number_of)
    crowded, usual = portions_of(number_of, rows * top, bound, slope, True), portions_of(number_of, rows * top, bound, slope, False)
    places = jnp.arange(number_of)

    def named(lengths, offset_by):
        used = int((lengths > 0).sum())
        fixed = max(1, used // 4)
        passed = fixed + (places - fixed + offset_by * (used - fixed)) % max(1, number_of - fixed)
        return jnp.zeros((number_of,), jnp.int32).at[ranking[jnp.where(places < fixed, places, passed)]].set(jnp.asarray(lengths, jnp.int32))

    lengths = jnp.where(number % 4 == 0, named(crowded, number // 4), named(usual, number - number // 4 - 1))
    mixed = jax.random.permutation(jax.random.fold_in(own, 3), number_of)
    source_of, sink = mixed[0:number_of // 2 * 2:2], mixed[1:number_of // 2 * 2:2]
    margin = jnp.minimum(lengths[source_of] - 1, bound - lengths[sink]) // 2
    margin = jnp.where((source_of == ranking[0]) | (sink == ranking[0]) | (lengths[sink] == 0), 0, jnp.maximum(margin, 0))
    passed = jax.random.randint(jax.random.fold_in(own, 4), (number_of // 2,), 0, 1 << 20) % (margin + 1)
    lengths = lengths.at[source_of].add(-passed).at[sink].add(passed)
    labels = jnp.searchsorted(jnp.cumsum(lengths), jnp.arange(rows * top), side="right").astype(jnp.int32)
    table = labels.reshape(top, rows).T
    table = table[jax.random.permutation(jax.random.fold_in(own, 1), rows)]
    offset_by = jax.random.randint(jax.random.fold_in(own, 2), (rows, 1), 0, top)
    return jnp.take_along_axis(table, (jnp.arange(top)[None, :] + offset_by) % top, axis=1)


def portions_of(number_of, total, bound, lean, full):
    portions = [(1 << 20) // math.isqrt(grade ** lean) + 1 for grade in range(1, number_of + 1)]
    largest = bound if full else min(bound, max(-(-total // number_of), total * portions[0] // sum(portions)))
    least = 1 if total - largest >= number_of - 1 else 0
    given, rest = [largest] + [least] * (number_of - 1), total - largest - least * (number_of - 1)
    while rest > 0:
        candidates = [i for i in range(1, number_of) if given[i] < largest] or [i for i in range(1, number_of) if given[i] < bound]
        pool, remaining = sum([portions[i] for i in candidates]), rest
        for i in candidates:
            more = min(bound - given[i], max(1, remaining * portions[i] // pool), rest)
            given[i] = given[i] + more
            rest = rest - more
    return np.array(given)


def setup_inputs(seed: int = 0, part: int = 0) -> dict:
    key_of = jax.random.split(jax.random.key(seed), 7)
    part_splits = jax.random.split(jax.random.fold_in(key_of[6], part), 7)
    particles = draw_particles(jax.random.fold_in(jax.random.fold_in(key_of[6], part), 71), part)
    projections = draw_projections(jax.random.fold_in(key_of[6], 71), part)
    ctf = jnp.clip(jax.random.uniform(key_of[2], (NDEF, PIX), jnp.float32, -1.0, 1.0), -1.0, 1.0).astype(jnp.bfloat16)
    defocus_group = set_ends(jax.random.randint(part_splits[3], (PARTICLES,), 0, NDEF), jax.random.fold_in(part_splits[3], 1), 0, NDEF - 1).astype(jnp.int32)
    offsets = set_ends(jax.random.randint(part_splits[4], (PARTICLES, 2), -8, 9), jax.random.fold_in(part_splits[4], 1), -8, 8).astype(jnp.int32)
    routes_keys = jax.random.split(jax.random.fold_in(part_splits[5], 1), PARTICLES // PART_DEV)
    routes_turns = jax.random.permutation(jax.random.fold_in(part_splits[5], 3), PARTICLES // PART_DEV)
    routes = jax.vmap(lambda own, number: deal_out(jax.random.fold_in(part_splits[5], 2), own, number, PART_DEV, N_ORIENT, TOPK, CAP, 2))(routes_keys, routes_turns).reshape((PARTICLES, TOPK))
    return dict(particles=particles, projections=projections, ctf=ctf, defocus_group=defocus_group, offsets=offsets, routes=routes)


two_pi = 2.0 * math.pi
highest = lax.Precision.HIGHEST
local_across = np.array([0, 1, -1, 0, 0], dtype=np.int32)
local_down = np.array([0, 0, 0, 1, -1], dtype=np.int32)


def frequencies():
    column = jnp.arange(KX * KY, dtype=jnp.int32)
    return column // KY, column % KY - KY // 2


def rotation(shift_across, shift_down, freq_across, freq_down):
    turns = jnp.mod(freq_across * shift_across + freq_down * shift_down, BOX)
    angle = turns.astype(jnp.float32) * (two_pi / BOX)
    return jnp.cos(angle), jnp.sin(angle)


def combine_stats(peaks, masses):
    top_value = jnp.max(peaks, axis=-1, keepdims=True)
    return top_value[..., 0] + jnp.log(jnp.sum(masses * jnp.exp(peaks - top_value), axis=-1))


def align_images(images, ctf_rows, shifts, freq_across, freq_down, pixel_count):
    real_part = images[:, :pixel_count].astype(jnp.float32)
    imag_part = images[:, pixel_count:].astype(jnp.float32)
    cos_base, sin_base = rotation(shifts[:, 0:1], shifts[:, 1:2], freq_across[None, :], freq_down[None, :])
    first = (real_part * cos_base + imag_part * sin_base) * ctf_rows
    second = (imag_part * cos_base - real_part * sin_base) * ctf_rows
    return jnp.concatenate([first, second], axis=1).astype(jnp.bfloat16)


def spread_phase(table, ndim_rest):
    return table.reshape((table.shape[0],) + (1,) * ndim_rest + (table.shape[1],))


def turn_refs(ref_block, cos_shift, sin_shift, pixel_count):
    real_ref = ref_block[..., :pixel_count].astype(jnp.float32)
    imag_ref = ref_block[..., pixel_count:].astype(jnp.float32)
    cos_wide = spread_phase(cos_shift, real_ref.ndim - 1)
    sin_wide = spread_phase(sin_shift, real_ref.ndim - 1)
    first = real_ref[None] * cos_wide - imag_ref[None] * sin_wide
    second = real_ref[None] * sin_wide + imag_ref[None] * cos_wide
    turned = jnp.concatenate([first, second], axis=-1).astype(jnp.bfloat16)
    return turned, real_ref * real_ref + imag_ref * imag_ref


def back_rotate(summed, cos_shift, sin_shift, pixel_count):
    cos_wide = spread_phase(cos_shift, summed.ndim - 2)
    sin_wide = spread_phase(sin_shift, summed.ndim - 2)
    real_sum = summed[..., :pixel_count]
    imag_sum = summed[..., pixel_count:]
    first = jnp.sum(real_sum * cos_wide + imag_sum * sin_wide, axis=0)
    second = jnp.sum(imag_sum * cos_wide - real_sum * sin_wide, axis=0)
    return jnp.concatenate([first, second], axis=-1)


def reference(particles, projections, ctf, defocus_group, offsets, routes):
    pixel_count = KX * KY
    freq_across, freq_down = frequencies()
    ctf_table = ctf.astype(jnp.float32)
    group_total = PARTICLES // PART_DEV

    def base_group(inputs):
        images, group_ids, shifts = inputs
        return align_images(images, ctf_table[group_ids], shifts, freq_across, freq_down, pixel_count)

    aligned = lax.map(base_group, (particles.reshape(group_total, PART_DEV, 2 * pixel_count),
                                   defocus_group.reshape(group_total, PART_DEV),
                                   offsets.reshape(group_total, PART_DEV, 2)))
    aligned = aligned.reshape(PARTICLES, 2 * pixel_count)
    cos_shift, sin_shift = rotation(jnp.asarray(local_across, dtype=jnp.int32)[:, None],
                                    jnp.asarray(local_down, dtype=jnp.int32)[:, None],
                                    freq_across[None, :], freq_down[None, :])
    real_all = projections[..., :pixel_count].astype(jnp.float32)
    imag_all = projections[..., pixel_count:].astype(jnp.float32)
    magnitude = real_all * real_all + imag_all * imag_all
    energy = jnp.einsum('gj,cdj->gcd', ctf_table * ctf_table, magnitude, precision=highest)
    row_of = (jnp.arange(PARTICLES, dtype=jnp.int32) // PART_DEV) % N_CLS
    flat_routes = routes.reshape(-1)
    flat_rows = jnp.repeat(row_of, TOPK)
    entry_total = PARTICLES * TOPK
    limit = CAP * N_ORIENT
    shift_total = cos_shift.shape[0]

    def block_scores(block_index):
        ref_block = lax.dynamic_slice_in_dim(projections, block_index * ORI_DEV, ORI_DEV, 1)
        turned, unused_mag = turn_refs(ref_block, cos_shift, sin_shift, pixel_count)
        turned_flat = turned.reshape(-1, 2 * pixel_count)
        block_energy = lax.dynamic_slice_in_dim(energy, block_index * ORI_DEV, ORI_DEV, 2)
        orders_all, occupied_all, scores_all = [], [], []
        for cls_row in range(N_CLS):
            matches = (flat_routes == block_index) & (flat_rows == cls_row)
            chosen_order = jnp.argsort(jnp.where(matches, 0, 1).astype(jnp.int32), stable=True)[:limit].astype(jnp.int32)
            occupied = matches[chosen_order].astype(jnp.float32)
            owners = chosen_order // TOPK
            rows_used = aligned[owners]
            products = lax.dot_general(rows_used, turned_flat, (((1,), (1,)), ((), ())), preferred_element_type=jnp.float32)
            slot_energy = block_energy[defocus_group[owners]]
            score = products.reshape(limit, shift_total, CLASSES, ORI_DEV) - 0.5 * slot_energy[:, None]
            orders_all.append(chosen_order)
            occupied_all.append(occupied)
            scores_all.append(score)
        return jnp.stack(orders_all), jnp.stack(occupied_all), jnp.stack(scores_all)

    orders, occupieds, scores = lax.map(block_scores, jnp.arange(N_ORIENT, dtype=jnp.int32))
    peaks = jnp.max(scores, axis=(3, 4, 5))
    masses = jnp.sum(jnp.exp(scores - peaks[..., None, None, None]), axis=(3, 4, 5))
    target = jnp.where(occupieds > 0, orders, entry_total).reshape(-1)
    entry_peak = jnp.zeros((entry_total,), jnp.float32).at[target].set(peaks.reshape(-1), mode="drop")
    entry_mass = jnp.zeros((entry_total,), jnp.float32).at[target].set(masses.reshape(-1), mode="drop")
    log_evidence = combine_stats(entry_peak.reshape(PARTICLES, TOPK), entry_mass.reshape(PARTICLES, TOPK))

    def block_sums(inputs):
        block_orders, block_occupied, block_scores_in = inputs
        running = jnp.zeros((CLASSES, ORI_DEV, 2 * pixel_count), jnp.float32)
        for cls_row in range(N_CLS):
            owners = block_orders[cls_row] // TOPK
            rows_used = aligned[owners]
            evidence = log_evidence[owners]
            live = (block_occupied[cls_row] > 0)[:, None, None, None]
            exponent = jnp.where(live, block_scores_in[cls_row] - evidence[:, None, None, None], 0.0)
            weights = jnp.where(live, jnp.exp(exponent), 0.0).astype(jnp.bfloat16)
            summed = lax.dot_general(weights.reshape(limit, -1), rows_used, (((0,), (0,)), ((), ())),
                                     preferred_element_type=jnp.float32)
            summed = summed.reshape(shift_total, CLASSES, ORI_DEV, 2 * pixel_count)
            partial_value = back_rotate(summed, cos_shift, sin_shift, pixel_count).astype(jnp.bfloat16)
            partial_value = lax.optimization_barrier(partial_value)
            running = running + partial_value.astype(jnp.float32)
        return running.astype(jnp.bfloat16)

    sums = lax.map(block_sums, (orders, occupieds, scores))
    data_sum = jnp.transpose(sums, (1, 0, 2, 3)).reshape(CLASSES, DIRECTIONS, 2 * pixel_count)
    return (log_evidence, data_sum)
```

```python
import math

import jax
import jax.numpy as jnp
import numpy as np
from jax import lax
from jax.experimental import pallas as pl
from jax.experimental.pallas import tpu as pltpu
from jax.sharding import PartitionSpec as P

KX = 86
KY = 192
BOX = 256


two_pi = 2.0 * math.pi
highest = lax.Precision.HIGHEST
local_across = np.array([0, 1, -1, 0, 0], dtype=np.int32)
local_down = np.array([0, 0, 0, 1, -1], dtype=np.int32)


def frequencies():
    column = jnp.arange(KX * KY, dtype=jnp.int32)
    return (column // KY, column % KY - KY // 2)


def rotation(shift_across, shift_down, freq_across, freq_down):
    turns = jnp.mod(freq_across * shift_across + freq_down * shift_down, BOX)
    angle = turns.astype(jnp.float32) * (two_pi / BOX)
    return (jnp.cos(angle), jnp.sin(angle))


def combine_stats(peaks, masses):
    top_value = jnp.max(peaks, axis=-1, keepdims=True)
    return top_value[..., 0] + jnp.log(jnp.sum(masses * jnp.exp(peaks - top_value), axis=-1))


def align_images(images, ctf_rows, shifts, freq_across, freq_down, pixel_count):
    real_part = images[:, :pixel_count].astype(jnp.float32)
    imag_part = images[:, pixel_count:].astype(jnp.float32)
    cos_base, sin_base = rotation(
        shifts[:, 0:1], shifts[:, 1:2], freq_across[None, :], freq_down[None, :]
    )
    first = (real_part * cos_base + imag_part * sin_base) * ctf_rows
    second = (imag_part * cos_base - real_part * sin_base) * ctf_rows
    return jnp.concatenate([first, second], axis=1).astype(jnp.bfloat16)


def spread_phase(table, ndim_rest):
    return table.reshape((table.shape[0],) + (1,) * ndim_rest + (table.shape[1],))


def turn_refs(ref_block, cos_shift, sin_shift, pixel_count):
    real_ref = ref_block[..., :pixel_count].astype(jnp.float32)
    imag_ref = ref_block[..., pixel_count:].astype(jnp.float32)
    cos_wide = spread_phase(cos_shift, real_ref.ndim - 1)
    sin_wide = spread_phase(sin_shift, real_ref.ndim - 1)
    first = real_ref[None] * cos_wide - imag_ref[None] * sin_wide
    second = real_ref[None] * sin_wide + imag_ref[None] * cos_wide
    turned = jnp.concatenate([first, second], axis=-1).astype(jnp.bfloat16)
    return (turned, real_ref * real_ref + imag_ref * imag_ref)


def back_rotate(summed, cos_shift, sin_shift, pixel_count):
    cos_wide = spread_phase(cos_shift, summed.ndim - 2)
    sin_wide = spread_phase(sin_shift, summed.ndim - 2)
    real_sum = summed[..., :pixel_count]
    imag_sum = summed[..., pixel_count:]
    first = jnp.sum(real_sum * cos_wide + imag_sum * sin_wide, axis=0)
    second = jnp.sum(imag_sum * cos_wide - real_sum * sin_wide, axis=0)
    return jnp.concatenate([first, second], axis=-1)


def slot_places(route_rows, orient_size):
    targets = route_rows.reshape(-1)
    onehot = (targets[:, None] == jnp.arange(orient_size, dtype=jnp.int32)[None, :]).astype(
        jnp.int32
    )
    place = jnp.arange(targets.shape[0], dtype=jnp.int32)
    earlier = (place[None, :] < place[:, None]).astype(jnp.float32)
    before = jnp.dot(earlier, onehot.astype(jnp.float32), precision=highest).astype(jnp.int32)
    return (targets, jnp.sum(before * onehot, axis=1))


def per_device_slots(particles, projections, ctf, defocus_group, offsets, routes):
    pixel_count = KX * KY
    own_count = particles.shape[0]
    route_count = routes.shape[1]
    class_local = projections.shape[0]
    directions = projections.shape[1]
    group_count = ctf.shape[0]
    orient_size = lax.axis_size("orient")
    capacity = max(2, (own_count * route_count + orient_size - 1) // orient_size)
    total_slots = orient_size * capacity
    freq_across, freq_down = frequencies()
    ctf_table = ctf.astype(jnp.float32)
    group_onehot = (
        defocus_group[:, None] == jnp.arange(group_count, dtype=jnp.int32)[None, :]
    ).astype(jnp.float32)
    ctf_rows = jnp.dot(group_onehot, ctf_table, precision=highest)
    aligned = align_images(particles, ctf_rows, offsets, freq_across, freq_down, pixel_count)
    targets, orders = slot_places(routes, orient_size)
    slot_ids = targets * capacity + orders
    matches = (slot_ids[None, :] == jnp.arange(total_slots, dtype=jnp.int32)[:, None]).astype(
        jnp.int32
    )
    picked = jnp.sum(matches.reshape(total_slots, own_count, route_count), axis=2)
    send_images = jnp.dot(picked.astype(jnp.bfloat16), aligned, preferred_element_type=jnp.float32)
    send_images = send_images.astype(jnp.bfloat16).reshape(orient_size, capacity, 2 * pixel_count)
    send_codes = jnp.sum(picked * (defocus_group + 1)[None, :], axis=1).reshape(
        orient_size, capacity
    )
    tiles, codes = (
        lax.all_to_all(send_images, "orient", split_axis=0, concat_axis=0, tiled=True),
        lax.all_to_all(send_codes, "orient", split_axis=0, concat_axis=0, tiled=True),
    )
    rows_in = tiles.reshape(total_slots, 2 * pixel_count)
    codes_in = codes.reshape(total_slots)
    slot_groups = (
        codes_in[:, None] - 1 == jnp.arange(group_count, dtype=jnp.int32)[None, :]
    ).astype(jnp.float32)
    occupied = codes_in > 0
    cos_shift, sin_shift = rotation(
        jnp.asarray(local_across, dtype=jnp.int32)[:, None],
        jnp.asarray(local_down, dtype=jnp.int32)[:, None],
        freq_across[None, :],
        freq_down[None, :],
    )
    shift_total = cos_shift.shape[0]
    ctf_square = ctf_table * ctf_table
    ref_piece = lax.all_gather(projections, "cls", axis=0, tiled=True)
    piece_rows = ref_piece.shape[0]
    group_size = 2
    grouped = ref_piece.reshape(piece_rows // group_size, group_size, directions, 2 * pixel_count)

    def one_group(ref_block):
        turned, magnitude = turn_refs(ref_block, cos_shift, sin_shift, pixel_count)
        products = lax.dot_general(
            rows_in,
            turned.reshape(-1, 2 * pixel_count),
            (((1,), (1,)), ((), ())),
            preferred_element_type=jnp.float32,
        )
        energy = lax.dot_general(
            ctf_square,
            magnitude.reshape(group_size * directions, pixel_count),
            (((1,), (1,)), ((), ())),
            precision=highest,
        )
        slot_energy = jnp.dot(slot_groups, energy, precision=highest).reshape(
            total_slots, 1, group_size, directions
        )
        return (
            products.reshape(total_slots, shift_total, group_size, directions) - 0.5 * slot_energy
        )

    stacked = lax.map(one_group, grouped)
    scores = jnp.transpose(stacked, (1, 2, 0, 3, 4)).reshape(
        total_slots, shift_total, piece_rows, directions
    )
    slot_peak = jnp.max(scores, axis=(1, 2, 3))
    slot_mass = jnp.sum(jnp.exp(scores - slot_peak[:, None, None, None]), axis=(1, 2, 3))
    back_peak, back_mass = (
        lax.all_to_all(
            slot_peak.reshape(orient_size, capacity),
            "orient",
            split_axis=0,
            concat_axis=0,
            tiled=True,
        ),
        lax.all_to_all(
            slot_mass.reshape(orient_size, capacity),
            "orient",
            split_axis=0,
            concat_axis=0,
            tiled=True,
        ),
    )
    match_table = matches.astype(jnp.float32)
    entry_peak = jnp.dot(back_peak.reshape(-1), match_table, precision=highest).reshape(
        own_count, route_count
    )
    entry_mass = jnp.dot(back_mass.reshape(-1), match_table, precision=highest).reshape(
        own_count, route_count
    )
    log_evidence = combine_stats(entry_peak, entry_mass)
    slot_value = jnp.dot(picked.astype(jnp.float32), log_evidence, precision=highest).reshape(
        orient_size, capacity
    )
    evidence_in = lax.all_to_all(
        slot_value, "orient", split_axis=0, concat_axis=0, tiled=True
    ).reshape(total_slots)
    live = occupied[:, None, None, None]
    exponent = jnp.where(live, scores - evidence_in[:, None, None, None], 0.0)
    weights = jnp.where(live, jnp.exp(exponent), 0.0).astype(jnp.bfloat16)
    class_group_size = 2

    def one_group(group_index):
        weight_part = lax.dynamic_slice_in_dim(
            weights, group_index * class_group_size, class_group_size, 2
        )
        summed = lax.dot_general(
            weight_part.reshape(total_slots, -1),
            rows_in,
            (((0,), (0,)), ((), ())),
            preferred_element_type=jnp.float32,
        )
        summed = summed.reshape(shift_total, class_group_size, directions, 2 * pixel_count)
        return back_rotate(summed, cos_shift, sin_shift, pixel_count)

    results = lax.map(
        one_group,
        jnp.arange(class_local * lax.axis_size("cls") // class_group_size, dtype=jnp.int32),
    )
    data_sum = lax.psum_scatter(
        results.reshape(class_local * lax.axis_size("cls"), directions, 2 * pixel_count).astype(
            jnp.bfloat16
        ),
        "cls",
        scatter_dimension=0,
        tiled=True,
    )
    return (log_evidence, data_sum)


MESH = pl.DeviceIdType.MESH
ANY = pl.BlockSpec(memory_space=pl.ANY)
VMEM_BYTES = 48 * 2**20
f32 = jnp.float32
bf16 = jnp.bfloat16


def place_of(group):
    o, c = lax.axis_index("orient"), lax.axis_index("cls")
    return o // group, o % group, c


def greet(peers):
    barrier = pltpu.get_barrier_semaphore()
    for peer in peers:
        pl.semaphore_signal(barrier, inc=1, device_id=peer, device_id_type=MESH)
    pl.semaphore_wait(barrier, len(peers))


def remote(src, dst, send, recv, peer):
    return pltpu.make_async_remote_copy(
        src_ref=src, dst_ref=dst, send_sem=send, recv_sem=recv,
        device_id=peer, device_id_type=MESH,
    )


def gather_kernel(group, n_cls, a_ref, p_ref, m_ref, a_out, p_out, m_out,
                  local, a_send, a_recv, m_send, m_recv, p_send, p_recv, q_send, q_recv, far_sem):
    hi, m, c = place_of(group)
    mates = [{"orient": hi * group + (m + s) % group, "cls": c} for s in range(1, group)]
    owners = [{"orient": hi * group + m, "cls": (c + s) % n_cls} for s in range(1, n_cls)]
    far = {"orient": (1 - hi) * group + m, "cls": c}
    greet(mates + owners + [far])
    far_copy = remote(p_ref, p_out.at[hi, c], far_sem.at[0], far_sem.at[1], far)
    far_copy.start()
    own = [
        pltpu.make_async_copy(a_ref, a_out.at[m], local.at[0]),
        pltpu.make_async_copy(p_ref, p_out.at[hi, c], local.at[1]),
        pltpu.make_async_copy(m_ref, m_out.at[m], local.at[2]),
    ]
    copies = []
    for s, peer in enumerate(owners):
        copies.append(remote(p_ref, p_out.at[hi, c], p_send.at[s], p_recv.at[s], peer))
    for s, peer in enumerate(mates):
        copies.append(remote(a_ref, a_out.at[m], a_send.at[s], a_recv.at[s], peer))
        copies.append(remote(m_ref, m_out.at[m], m_send.at[s], m_recv.at[s], peer))
    for copy in copies + own:
        copy.start()
    far_copy.wait_recv()
    there = p_out.at[1 - hi, c]
    passed = [remote(there, there, q_send.at[s], q_recv.at[s], peer) for s, peer in enumerate(owners)]
    for copy in passed:
        copy.start()
    for copy in own:
        copy.wait()
    for copy in copies + passed:
        copy.wait()
    far_copy.wait_send()


def share_kernel(group, s_ref, s_out, local, send, recv):
    hi, m, c = place_of(group)
    mates = [{"orient": hi * group + (m + s) % group, "cls": c} for s in range(1, group)]
    greet(mates)
    own = pltpu.make_async_copy(s_ref, s_out.at[m], local.at[0])
    copies = [remote(s_ref, s_out.at[m], send.at[s], recv.at[s], peer) for s, peer in enumerate(mates)]
    for copy in copies + [own]:
        copy.start()
    for copy in copies + [own]:
        copy.wait()


def reduce_kernel(group, n_cls, u_ref, out_ref, land, send_far, land_far,
                  near_send, near_recv, away_send, away_recv, far_sem):
    hi, m, c = place_of(group)
    owners = [{"orient": hi * group + m, "cls": (c + s) % n_cls} for s in range(1, n_cls)]
    far = {"orient": (1 - hi) * group + m, "cls": c}
    greet(owners + [far])
    away, near = [], []
    for s in range(1, n_cls):
        to = (c + s) % n_cls
        away.append(remote(u_ref.at[1 - hi, to], land.at[1, s - 1], away_send.at[s - 1], away_recv.at[s - 1], owners[s - 1]))
        near.append(remote(u_ref.at[hi, to], land.at[0, s - 1], near_send.at[s - 1], near_recv.at[s - 1], owners[s - 1]))
    for copy in away + near:
        copy.start()
    for copy in away:
        copy.wait_recv()
    total = u_ref[1 - hi, c].astype(f32)
    for s in range(n_cls - 1):
        total += land[1, s].astype(f32)
    send_far[...] = total.astype(bf16)
    far_copy = remote(send_far, land_far, far_sem.at[0], far_sem.at[1], far)
    far_copy.start()
    for copy in near:
        copy.wait_recv()
    total = u_ref[hi, c].astype(f32)
    for s in range(n_cls - 1):
        total += land[0, s].astype(f32)
    far_copy.wait_recv()
    out_ref[...] = (total + land_far[...].astype(f32)).astype(bf16)
    for copy in away + near:
        copy.wait_send()
    far_copy.wait_send()


def score_kernel(a_ref, p_ref, ctf_ref, tab_ref, full_ref, energy_ref, re, im):
    halves, n_cls, twice, width = p_ref.shape
    classes = twice // 2
    for h in range(halves):
        for k in range(n_cls):
            at = (h * n_cls + k) * classes
            block = p_ref[h, k].astype(f32)
            re[at : at + classes] = block[:classes]
            im[at : at + classes] = block[classes:]
    p, q = re[...], im[...]
    square = ctf_ref[...].astype(f32)
    energy = lax.dot_general(
        square * square, p * p + q * q, (((1,), (1,)), ((), ())),
        precision=highest, preferred_element_type=f32,
    )
    rows = []
    for turn in range(5):
        if turn == 0:
            rows += [p.astype(bf16), q.astype(bf16)]
            continue
        axis = (turn - 1) // 2
        cos, sin = tab_ref[axis : axis + 1], tab_ref[2 + axis : 3 + axis]
        sin = sin if turn % 2 else -sin
        rows += [(p * cos - q * sin).astype(bf16), (p * sin + q * cos).astype(bf16)]
    turned = jnp.concatenate(rows, axis=0)
    images = jnp.concatenate([a_ref[s] for s in range(a_ref.shape[0])], axis=0)
    full = lax.dot_general(turned, images, (((1,), (1,)), ((), ())), preferred_element_type=f32)

    @pl.when(pl.program_id(0) == 0)
    def _():
        full_ref[...] = jnp.zeros_like(full_ref)
        energy_ref[...] = jnp.zeros_like(energy_ref)

    full_ref[...] += full
    energy_ref[...] += energy


def sum_kernel(w_ref, a_ref, tab_ref, u_ref):
    halves, n_cls, twice, width = u_ref.shape
    classes = twice // 2
    n = halves * n_cls * classes
    images = jnp.concatenate([a_ref[s] for s in range(a_ref.shape[0])], axis=0)
    summed = jnp.dot(w_ref[...], images, preferred_element_type=f32)
    first, second = summed[:n], summed[n : 2 * n]
    for turn in range(1, 5):
        axis = (turn - 1) // 2
        cos, sin = tab_ref[axis : axis + 1], tab_ref[2 + axis : 3 + axis]
        sin = sin if turn % 2 else -sin
        real, imag = summed[2 * n * turn : 2 * n * turn + n], summed[2 * n * turn + n : 2 * n * (turn + 1)]
        first += real * cos + imag * sin
        second += imag * cos - real * sin
    for h in range(halves):
        for k in range(n_cls):
            at = (h * n_cls + k) * classes
            u_ref[h, k, :classes] = first[at : at + classes].astype(bf16)
            u_ref[h, k, classes:] = second[at : at + classes].astype(bf16)


def local_tables():
    j = np.arange(KX * KY)
    angles = np.stack([j // KY, j % KY - KY // 2]) * (two_pi / BOX)
    return np.concatenate([np.cos(angles), np.sin(angles)]).astype(np.float32)


def column_block(pixel_count):
    lanes = pixel_count // 128
    return 128 * max(d for d in range(1, lanes + 1) if lanes % d == 0 and d <= 48)


def per_device_halves(group, particles, projections, ctf, defocus_group, offsets, routes):
    pix = KX * KY
    own = particles.shape[0]
    classes = projections.shape[0]
    n_groups = ctf.shape[0]
    n_orient, n_cls = lax.axis_size("orient"), lax.axis_size("cls")
    hi, m, c = place_of(group)
    tables = jnp.asarray(local_tables())
    freq_across, freq_down = frequencies()
    group_onehot = (defocus_group[:, None] == jnp.arange(n_groups, dtype=jnp.int32)[None, :]).astype(bf16)
    ctf_rows = jnp.dot(group_onehot, ctf, preferred_element_type=f32)
    cos_a, sin_a = rotation(offsets[:, 0:1], jnp.zeros_like(offsets[:, 1:2]), jnp.arange(KX)[None, :], 0)
    cos_b, sin_b = rotation(offsets[:, 1:2], jnp.zeros_like(offsets[:, 1:2]), jnp.arange(KY)[None, :] - KY // 2, 0)
    turns = jnp.mod(freq_across[None, :] * offsets[:, 0:1] + freq_down[None, :] * offsets[:, 1:2], BOX)
    angle = turns.astype(f32) * (two_pi / BOX)
    cos_base, sin_base = jnp.cos(angle), jnp.sin(angle)
    real_part = particles[:, :pix].astype(f32)
    imag_part = particles[:, pix:].astype(f32)
    first = (real_part * cos_base + imag_part * sin_base) * ctf_rows
    second = (imag_part * cos_base - real_part * sin_base) * ctf_rows
    aligned = jnp.concatenate([first, second], axis=0).astype(bf16)
    own_refs = projections.reshape(classes, 2, pix).transpose(1, 0, 2).reshape(2 * classes, pix)
    listed = jnp.any(routes.T[:, None, :] == jnp.arange(n_orient, dtype=jnp.int32)[None, :, None], axis=0)
    meta = jnp.concatenate([listed.astype(f32), defocus_group.astype(f32)[None, :]], axis=0)
    meta = jnp.pad(meta, ((0, -meta.shape[0] % 8), (0, 128 - own)))
    halves = n_orient // group
    dma = pltpu.SemaphoreType.DMA
    images, refs, metas = pl.pallas_call(
        lambda *r: gather_kernel(group, n_cls, *r),
        out_shape=(
            jax.ShapeDtypeStruct((group,) + aligned.shape, bf16),
            jax.ShapeDtypeStruct((halves, n_cls) + own_refs.shape, bf16),
            jax.ShapeDtypeStruct((group,) + meta.shape, f32),
        ),
        in_specs=[ANY] * 3,
        out_specs=(ANY,) * 3,
        scratch_shapes=[dma((3,))] + [dma((group - 1,))] * 4 + [dma((n_cls - 1,))] * 4 + [dma((2,))],
        compiler_params=pltpu.CompilerParams(collective_id=0, has_side_effects=True),
    )(aligned, own_refs, meta)

    block = column_block(pix)
    steps = pix // block
    kd = halves * n_cls * classes
    rows = 5 * 2 * kd
    wide = group * 2 * own
    image_spec = pl.BlockSpec((group, 2 * own, block), lambda i: (0, 0, i))
    table_spec = pl.BlockSpec((4, block), lambda i: (0, i))
    stack_spec = pl.BlockSpec((halves, n_cls, 2 * classes, block), lambda i: (0, 0, 0, i))
    full, energy = pl.pallas_call(
        score_kernel,
        grid=(steps,),
        out_shape=(jax.ShapeDtypeStruct((rows, wide), f32), jax.ShapeDtypeStruct((n_groups, kd), f32)),
        in_specs=[image_spec, stack_spec, pl.BlockSpec((n_groups, block), lambda i: (0, i)), table_spec],
        out_specs=(pl.BlockSpec((rows, wide), lambda i: (0, 0)), pl.BlockSpec((n_groups, kd), lambda i: (0, 0))),
        scratch_shapes=[pltpu.VMEM((kd, block), f32)] * 2,
        compiler_params=pltpu.CompilerParams(vmem_limit_bytes=VMEM_BYTES),
    )(images, refs, ctf, tables)

    full = full.reshape(5, 2, kd, group, 2, own)
    scores = full[:, 0, :, :, 0] + full[:, 1, :, :, 1]
    groups_of = metas[:, n_orient, :own]
    onehot = (groups_of[:, :, None] == jnp.arange(n_groups, dtype=f32)).astype(f32)
    scores = scores - 0.5 * jnp.einsum("sig,gk->ksi", onehot, energy, precision=highest)[None]
    mine = jnp.stack([lax.dynamic_index_in_dim(metas, h * group + m, 1, False)[:, :own] for h in range(halves)])
    live = jnp.repeat(mine > 0, n_cls * classes, axis=0)[None]
    masked = jnp.where(live, scores, -jnp.inf)
    peak = jnp.max(masked, axis=(0, 1))
    safe = jnp.where(jnp.any(mine > 0, axis=0), peak, -3e38)
    mass = jnp.sum(jnp.where(live, jnp.exp(jnp.where(live, scores - safe, 0.0)), 0.0), axis=(0, 1))
    stats = jnp.stack([safe, mass]).reshape(2, group * own)
    stats = jnp.pad(stats, ((0, 6), (0, 128 - group * own)))
    shared = pl.pallas_call(
        lambda *r: share_kernel(group, *r),
        out_shape=jax.ShapeDtypeStruct((group, 8, 128), f32),
        in_specs=[ANY],
        out_specs=ANY,
        scratch_shapes=[dma((1,)), dma((group - 1,)), dma((group - 1,))],
        compiler_params=pltpu.CompilerParams(collective_id=1, has_side_effects=True),
    )(stats)
    peaks, masses = shared[:, 0, : group * own], shared[:, 1, : group * own]
    top = jnp.max(peaks, axis=0)
    evidence = (top + jnp.log(jnp.sum(masses * jnp.exp(peaks - top), axis=0))).reshape(group, own)
    log_evidence = lax.dynamic_index_in_dim(evidence, m, 0, False)
    weight = jnp.where(live, jnp.exp(jnp.where(live, scores - evidence, 0.0)), 0.0).astype(bf16)
    zero = jnp.zeros_like(weight)
    spread = jnp.stack([jnp.stack([weight, zero], axis=3), jnp.stack([zero, weight], axis=3)], axis=1)
    sums = pl.pallas_call(
        sum_kernel,
        grid=(steps,),
        out_shape=jax.ShapeDtypeStruct(refs.shape, bf16),
        in_specs=[pl.BlockSpec((rows, wide), lambda i: (0, 0)), image_spec, table_spec],
        out_specs=stack_spec,
        compiler_params=pltpu.CompilerParams(vmem_limit_bytes=VMEM_BYTES),
    )(spread.reshape(rows, wide), images, tables)

    VM = pl.BlockSpec(memory_space=pltpu.VMEM)
    piece = (2 * classes, pix)
    out = pl.pallas_call(
        lambda *r: reduce_kernel(group, n_cls, *r),
        out_shape=jax.ShapeDtypeStruct(piece, bf16),
        in_specs=[VM],
        out_specs=VM,
        scratch_shapes=[pltpu.VMEM((2, n_cls - 1) + piece, bf16), pltpu.VMEM(piece, bf16), pltpu.VMEM(piece, bf16)]
        + [dma((n_cls - 1,))] * 4 + [dma((2,))],
        compiler_params=pltpu.CompilerParams(collective_id=2, has_side_effects=True, vmem_limit_bytes=VMEM_BYTES),
    )(sums)
    data_sum = out.reshape(2, classes, pix).transpose(1, 0, 2).reshape(classes, 1, 2 * pix)
    return (log_evidence, data_sum)


def solution(mesh):
    placed = (
        P(("groups", "orient", "cls"), None),
        P("cls", "orient", None),
        P(),
        P(("groups", "orient", "cls")),
        P(("groups", "orient", "cls"), None),
        P(("groups", "orient", "cls"), None),
    )

    def per_device(particles, projections, *rest):
        group = mesh.shape["orient"] // 2
        held = 2 * particles.size * group
        fits = mesh.shape["orient"] == 2 * group and group > 1 and mesh.shape["cls"] > 1
        fits = fits and 4 * held <= VMEM_BYTES and group * particles.shape[0] <= 128
        fits = fits and projections.shape[1] == 1
        if fits:
            return per_device_halves(group, particles, projections, *rest)
        return per_device_slots(particles, projections, *rest)

    return jax.shard_map(
        per_device,
        mesh=mesh,
        in_specs=placed,
        out_specs=(P(("groups", "orient", "cls")), P(("groups", "cls"), "orient", None)),
        check_vma=False,
    )
```

```python
import functools
import math

import jax
import jax.numpy as jnp
import numpy as np
from jax import lax
from jax.experimental import pallas as pl
from jax.experimental.pallas import tpu as pltpu
from jax.sharding import PartitionSpec as P

KX = 86
KY = 192
BOX = 256


two_pi = 2.0 * math.pi
highest = lax.Precision.HIGHEST
local_across = np.array([0, 1, -1, 0, 0], dtype=np.int32)
local_down = np.array([0, 0, 0, 1, -1], dtype=np.int32)


def frequencies():
    column = jnp.arange(KX * KY, dtype=jnp.int32)
    return (column // KY, column % KY - KY // 2)


def rotation(shift_across, shift_down, freq_across, freq_down):
    turns = jnp.mod(freq_across * shift_across + freq_down * shift_down, BOX)
    angle = turns.astype(jnp.float32) * (two_pi / BOX)
    return (jnp.cos(angle), jnp.sin(angle))


def combine_stats(peaks, masses):
    top_value = jnp.max(peaks, axis=-1, keepdims=True)
    return top_value[..., 0] + jnp.log(jnp.sum(masses * jnp.exp(peaks - top_value), axis=-1))


def align_images(images, ctf_rows, shifts, freq_across, freq_down, pixel_count):
    real_part = images[:, :pixel_count].astype(jnp.float32)
    imag_part = images[:, pixel_count:].astype(jnp.float32)
    cos_base, sin_base = rotation(
        shifts[:, 0:1], shifts[:, 1:2], freq_across[None, :], freq_down[None, :]
    )
    first = (real_part * cos_base + imag_part * sin_base) * ctf_rows
    second = (imag_part * cos_base - real_part * sin_base) * ctf_rows
    return jnp.concatenate([first, second], axis=1).astype(jnp.bfloat16)


def spread_phase(table, ndim_rest):
    return table.reshape((table.shape[0],) + (1,) * ndim_rest + (table.shape[1],))


def turn_refs(ref_block, cos_shift, sin_shift, pixel_count):
    real_ref = ref_block[..., :pixel_count].astype(jnp.float32)
    imag_ref = ref_block[..., pixel_count:].astype(jnp.float32)
    cos_wide = spread_phase(cos_shift, real_ref.ndim - 1)
    sin_wide = spread_phase(sin_shift, real_ref.ndim - 1)
    first = real_ref[None] * cos_wide - imag_ref[None] * sin_wide
    second = real_ref[None] * sin_wide + imag_ref[None] * cos_wide
    turned = jnp.concatenate([first, second], axis=-1).astype(jnp.bfloat16)
    return (turned, real_ref * real_ref + imag_ref * imag_ref)


def back_rotate(summed, cos_shift, sin_shift, pixel_count):
    cos_wide = spread_phase(cos_shift, summed.ndim - 2)
    sin_wide = spread_phase(sin_shift, summed.ndim - 2)
    real_sum = summed[..., :pixel_count]
    imag_sum = summed[..., pixel_count:]
    first = jnp.sum(real_sum * cos_wide + imag_sum * sin_wide, axis=0)
    second = jnp.sum(imag_sum * cos_wide - real_sum * sin_wide, axis=0)
    return jnp.concatenate([first, second], axis=-1)


def slot_places(route_rows, orient_size):
    targets = route_rows.reshape(-1)
    onehot = (targets[:, None] == jnp.arange(orient_size, dtype=jnp.int32)[None, :]).astype(
        jnp.int32
    )
    place = jnp.arange(targets.shape[0], dtype=jnp.int32)
    earlier = (place[None, :] < place[:, None]).astype(jnp.float32)
    before = jnp.dot(earlier, onehot.astype(jnp.float32), precision=highest).astype(jnp.int32)
    return (targets, jnp.sum(before * onehot, axis=1))


def per_device_slots(particles, projections, ctf, defocus_group, offsets, routes):
    pixel_count = KX * KY
    own_count = particles.shape[0]
    route_count = routes.shape[1]
    class_local = projections.shape[0]
    directions = projections.shape[1]
    group_count = ctf.shape[0]
    orient_size = lax.axis_size("orient")
    capacity = max(2, (own_count * route_count + orient_size - 1) // orient_size)
    total_slots = orient_size * capacity
    freq_across, freq_down = frequencies()
    ctf_table = ctf.astype(jnp.float32)
    group_onehot = (
        defocus_group[:, None] == jnp.arange(group_count, dtype=jnp.int32)[None, :]
    ).astype(jnp.float32)
    ctf_rows = jnp.dot(group_onehot, ctf_table, precision=highest)
    aligned = align_images(particles, ctf_rows, offsets, freq_across, freq_down, pixel_count)
    targets, orders = slot_places(routes, orient_size)
    slot_ids = targets * capacity + orders
    matches = (slot_ids[None, :] == jnp.arange(total_slots, dtype=jnp.int32)[:, None]).astype(
        jnp.int32
    )
    picked = jnp.sum(matches.reshape(total_slots, own_count, route_count), axis=2)
    send_images = jnp.dot(picked.astype(jnp.bfloat16), aligned, preferred_element_type=jnp.float32)
    send_images = send_images.astype(jnp.bfloat16).reshape(orient_size, capacity, 2 * pixel_count)
    send_codes = jnp.sum(picked * (defocus_group + 1)[None, :], axis=1).reshape(
        orient_size, capacity
    )
    tiles, codes = (
        lax.all_to_all(send_images, "orient", split_axis=0, concat_axis=0, tiled=True),
        lax.all_to_all(send_codes, "orient", split_axis=0, concat_axis=0, tiled=True),
    )
    rows_in = tiles.reshape(total_slots, 2 * pixel_count)
    codes_in = codes.reshape(total_slots)
    slot_groups = (
        codes_in[:, None] - 1 == jnp.arange(group_count, dtype=jnp.int32)[None, :]
    ).astype(jnp.float32)
    occupied = codes_in > 0
    cos_shift, sin_shift = rotation(
        jnp.asarray(local_across, dtype=jnp.int32)[:, None],
        jnp.asarray(local_down, dtype=jnp.int32)[:, None],
        freq_across[None, :],
        freq_down[None, :],
    )
    shift_total = cos_shift.shape[0]
    ctf_square = ctf_table * ctf_table
    ref_piece = lax.all_gather(projections, "cls", axis=0, tiled=True)
    piece_rows = ref_piece.shape[0]
    group_size = 2
    grouped = ref_piece.reshape(piece_rows // group_size, group_size, directions, 2 * pixel_count)

    def one_group(ref_block):
        turned, magnitude = turn_refs(ref_block, cos_shift, sin_shift, pixel_count)
        products = lax.dot_general(
            rows_in,
            turned.reshape(-1, 2 * pixel_count),
            (((1,), (1,)), ((), ())),
            preferred_element_type=jnp.float32,
        )
        energy = lax.dot_general(
            ctf_square,
            magnitude.reshape(group_size * directions, pixel_count),
            (((1,), (1,)), ((), ())),
            precision=highest,
        )
        slot_energy = jnp.dot(slot_groups, energy, precision=highest).reshape(
            total_slots, 1, group_size, directions
        )
        return (
            products.reshape(total_slots, shift_total, group_size, directions) - 0.5 * slot_energy
        )

    stacked = lax.map(one_group, grouped)
    scores = jnp.transpose(stacked, (1, 2, 0, 3, 4)).reshape(
        total_slots, shift_total, piece_rows, directions
    )
    slot_peak = jnp.max(scores, axis=(1, 2, 3))
    slot_mass = jnp.sum(jnp.exp(scores - slot_peak[:, None, None, None]), axis=(1, 2, 3))
    back_peak, back_mass = (
        lax.all_to_all(
            slot_peak.reshape(orient_size, capacity),
            "orient",
            split_axis=0,
            concat_axis=0,
            tiled=True,
        ),
        lax.all_to_all(
            slot_mass.reshape(orient_size, capacity),
            "orient",
            split_axis=0,
            concat_axis=0,
            tiled=True,
        ),
    )
    match_table = matches.astype(jnp.float32)
    entry_peak = jnp.dot(back_peak.reshape(-1), match_table, precision=highest).reshape(
        own_count, route_count
    )
    entry_mass = jnp.dot(back_mass.reshape(-1), match_table, precision=highest).reshape(
        own_count, route_count
    )
    log_evidence = combine_stats(entry_peak, entry_mass)
    slot_value = jnp.dot(picked.astype(jnp.float32), log_evidence, precision=highest).reshape(
        orient_size, capacity
    )
    evidence_in = lax.all_to_all(
        slot_value, "orient", split_axis=0, concat_axis=0, tiled=True
    ).reshape(total_slots)
    live = occupied[:, None, None, None]
    exponent = jnp.where(live, scores - evidence_in[:, None, None, None], 0.0)
    weights = jnp.where(live, jnp.exp(exponent), 0.0).astype(jnp.bfloat16)
    class_group_size = 2

    def one_group(group_index):
        weight_part = lax.dynamic_slice_in_dim(
            weights, group_index * class_group_size, class_group_size, 2
        )
        summed = lax.dot_general(
            weight_part.reshape(total_slots, -1),
            rows_in,
            (((0,), (0,)), ((), ())),
            preferred_element_type=jnp.float32,
        )
        summed = summed.reshape(shift_total, class_group_size, directions, 2 * pixel_count)
        return back_rotate(summed, cos_shift, sin_shift, pixel_count)

    results = lax.map(
        one_group,
        jnp.arange(class_local * lax.axis_size("cls") // class_group_size, dtype=jnp.int32),
    )
    data_sum = lax.psum_scatter(
        results.reshape(class_local * lax.axis_size("cls"), directions, 2 * pixel_count).astype(
            jnp.bfloat16
        ),
        "cls",
        scatter_dimension=0,
        tiled=True,
    )
    return (log_evidence, data_sum)


MESH = pl.DeviceIdType.MESH
VMEM_BYTES = 48 * 2**20
f32 = jnp.float32
bf16 = jnp.bfloat16


def place_of(group):
    o, c = lax.axis_index("orient"), lax.axis_index("cls")
    return o // group, o % group, c


def greet(peers):
    barrier = pltpu.get_barrier_semaphore()
    for peer in peers:
        pl.semaphore_signal(barrier, inc=1, device_id=peer, device_id_type=MESH)
    pl.semaphore_wait(barrier, len(peers))


def remote(src, dst, send, recv, peer):
    return pltpu.make_async_remote_copy(
        src_ref=src, dst_ref=dst, send_sem=send, recv_sem=recv,
        device_id=peer, device_id_type=MESH,
    )


def turn_of(tables, turn, columns):
    axis = (turn - 1) // 2
    cos, sin = tables[axis : axis + 1, columns], tables[2 + axis : 3 + axis, columns]
    return cos, (sin if turn % 2 else -sin)


def fused_kernel(group, n_cls, own, pieces,
                 a_ref, p_ref, m_ref, ctf_ref, tables,
                 sum_out, evidence_out,
                 images, refs, metas, re, im, full, stats, sums, land, send_far, land_far,
                 x_send, x_recv, s_send, s_recv, f_send, f_recv, m_send, m_recv,
                 p_send, p_recv, q_send, q_recv, far_sem, e_send, e_recv,
                 near_send, near_recv, away_send, away_recv, back_sem, local):
    hi, m, c = place_of(group)
    pix = a_ref.shape[1]
    width = pix // pieces
    classes = p_ref.shape[0] // 2
    n_groups = ctf_ref.shape[0]
    kd = 2 * n_cls * classes
    used = 2 * own * group
    sibling = m + 1 - 2 * (m % 2)
    at = lambda member: {"orient": hi * group + member, "cls": c}
    mates = [at((m + s) % group) for s in range(1, group)]
    hops = group // 2 - 1
    owners = [{"orient": hi * group + m, "cls": (c + s) % n_cls} for s in range(1, n_cls)]
    far = {"orient": (1 - hi) * group + m, "cls": c}
    greet(mates + owners + [far])

    far_copy = remote(p_ref, refs.at[hi, c], far_sem.at[0], far_sem.at[1], far)
    far_copy.start()
    kept = [
        pltpu.make_async_copy(a_ref, images.at[m], local.at[0]),
        pltpu.make_async_copy(p_ref, refs.at[hi, c], local.at[1]),
        pltpu.make_async_copy(m_ref, metas.at[m], local.at[2]),
    ]
    first = [remote(p_ref, refs.at[hi, c], p_send.at[s], p_recv.at[s], peer) for s, peer in enumerate(owners)]
    cols = [pl.ds(q * width, width) for q in range(pieces)]
    crossing, beside, onward = [], [], []
    for q in range(pieces):
        for k in range(hops):
            crossing.append(remote(a_ref.at[:, cols[q]], images.at[m, :, cols[q]], x_send.at[q, k], x_recv.at[q, k],
                                   at((m + 2 * (k + 1)) % group)))
            slot = images.at[(m + group - 2 * (k + 1)) % group, :, cols[q]]
            onward.append(remote(slot, slot, f_send.at[q, k], f_recv.at[q, k], at(sibling)))
        beside.append(remote(a_ref.at[:, cols[q]], images.at[m, :, cols[q]], s_send.at[q], s_recv.at[q], at(sibling)))
    told = [remote(m_ref, metas.at[m], m_send.at[s], m_recv.at[s], peer) for s, peer in enumerate(mates)]
    for copy in crossing + first + beside + told + kept:
        copy.start()
    far_copy.wait_recv()
    there = refs.at[1 - hi, c]
    passed = [remote(there, there, q_send.at[s], q_recv.at[s], peer) for s, peer in enumerate(owners)]
    for copy in passed:
        copy.start()
    full[...] = jnp.zeros_like(full)
    for copy in kept:
        copy.wait()
    for copy in first + passed:
        copy.wait_recv()

    def all_images(q):
        return jnp.concatenate([images[s, :, q * width : (q + 1) * width] for s in range(group)], axis=0)

    def score_piece(q):
        here = slice(q * width, (q + 1) * width)
        for h in range(2):
            for k in range(n_cls):
                row = (h * n_cls + k) * classes
                block = refs[h, k, :, here].astype(f32)
                re[row : row + classes] = block[:classes]
                im[row : row + classes] = block[classes:]
        p, q_ = re[...], im[...]
        square = ctf_ref[:, here].astype(f32)
        energy = lax.dot_general(p * p + q_ * q_, square * square, (((1,), (1,)), ((), ())),
                                 precision=highest, preferred_element_type=f32)
        rows = [p.astype(bf16), q_.astype(bf16)]
        for turn in range(1, 5):
            cos, sin = turn_of(tables, turn, here)
            rows += [(p * cos - q_ * sin).astype(bf16), (p * sin + q_ * cos).astype(bf16)]
        turned = jnp.concatenate(rows, axis=0)
        for copy in onward[q * hops : (q + 1) * hops] + [beside[q]]:
            copy.wait_recv()
        full[:, :used] += lax.dot_general(turned, all_images(q), (((1,), (1,)), ((), ())), preferred_element_type=f32)
        return energy

    energy = jnp.zeros((kd, n_groups), f32)
    for q in range(pieces):
        for copy, pass_on in zip(crossing[q * hops : (q + 1) * hops], onward[q * hops : (q + 1) * hops]):
            copy.wait_recv()
            pass_on.start()
        if q:
            energy += score_piece(q - 1)
    energy += score_piece(pieces - 1)
    for copy in told:
        copy.wait_recv()

    lanes = full.shape[1]
    meta = metas[0]
    for s in range(1, group):
        meta += pltpu.roll(metas[s], 2 * own * s, 1)
    n_orient = 2 * group
    listed, onehot = meta[:n_orient], meta[n_orient : n_orient + n_groups]
    level = jnp.dot(energy, onehot, precision=highest, preferred_element_type=f32)
    row_of = lax.broadcasted_iota(jnp.int32, listed.shape, 0)
    mine = [jnp.sum(jnp.where(row_of == h * group + m, listed, 0.0), axis=0, keepdims=True) for h in range(2)]
    live = jnp.concatenate([jnp.broadcast_to(row, (kd // 2, lanes)) for row in mine], axis=0) > 0
    score = []
    for turn in range(5):
        real, imag = full[2 * kd * turn : 2 * kd * turn + kd], full[2 * kd * turn + kd : 2 * kd * (turn + 1)]
        score.append(real + pltpu.roll(imag, lanes - own, 1) - 0.5 * level)
    low = -3.0e38
    peak = functools.reduce(jnp.maximum, score)
    peak = jnp.max(jnp.where(live, peak, low), axis=0, keepdims=True)
    mass = sum(jnp.where(live, jnp.exp(jnp.where(live, v - peak, 0.0)), 0.0) for v in score)
    mass = jnp.sum(mass, axis=0, keepdims=True)
    half_row = lax.broadcasted_iota(jnp.int32, (8, lanes), 0)
    stats[m] = jnp.where(half_row == 0, peak, jnp.where(half_row == 1, mass, 0.0))
    shared = [remote(stats.at[m], stats.at[m], e_send.at[s], e_recv.at[s], peer) for s, peer in enumerate(mates)]
    for copy in shared:
        copy.start()
    for copy in shared:
        copy.wait_recv()
    held = [stats[s] for s in range(group)]
    top = functools.reduce(jnp.maximum, [v[0:1] for v in held])
    evidence = top + jnp.log(sum(v[1:2] * jnp.exp(v[0:1] - top) for v in held))
    result = jnp.zeros((8, lanes), f32)
    wide = jnp.broadcast_to(evidence, (8, lanes))
    for s in range(group):
        moved = pltpu.roll(wide, lanes - 2 * own * s, 1) if s else wide
        result = jnp.where(m == s, moved, result)
    evidence_out[...] = result
    weights = []
    for value in score:
        weight = jnp.where(live, jnp.exp(jnp.where(live, value - evidence, 0.0)), 0.0)
        weights += [weight.astype(bf16), pltpu.roll(weight, own, 1).astype(bf16)]
    weights = jnp.concatenate(weights, axis=0)[:, :used]

    away, near = [], []
    for s in range(1, n_cls):
        to = (c + s) % n_cls
        away.append(remote(sums.at[1 - hi, to], land.at[1, s - 1], away_send.at[s - 1], away_recv.at[s - 1], owners[s - 1]))
        near.append(remote(sums.at[hi, to], land.at[0, s - 1], near_send.at[s - 1], near_recv.at[s - 1], owners[s - 1]))
    for q in range(pieces):
        here = slice(q * width, (q + 1) * width)
        summed = jnp.dot(weights, all_images(q), preferred_element_type=f32)
        real_sum, imag_sum = summed[:kd], summed[kd : 2 * kd]
        for turn in range(1, 5):
            cos, sin = turn_of(tables, turn, here)
            real, imag = summed[2 * kd * turn : 2 * kd * turn + kd], summed[2 * kd * turn + kd : 2 * kd * (turn + 1)]
            real_sum += real * cos + imag * sin
            imag_sum += imag * cos - real * sin
        for h in range(2):
            for k in range(n_cls):
                row = (h * n_cls + k) * classes
                sums[h, k, :classes, here] = real_sum[row : row + classes].astype(bf16)
                sums[h, k, classes:, here] = imag_sum[row : row + classes].astype(bf16)
    for copy in away + near:
        copy.start()
    for copy in away:
        copy.wait_recv()
    total = sums[1 - hi, c].astype(f32)
    for s in range(n_cls - 1):
        total += land[1, s].astype(f32)
    send_far[...] = total.astype(bf16)
    back = remote(send_far, land_far, back_sem.at[0], back_sem.at[1], far)
    back.start()
    for copy in near:
        copy.wait_recv()
    total = sums[hi, c].astype(f32)
    for s in range(n_cls - 1):
        total += land[0, s].astype(f32)
    back.wait_recv()
    sum_out[...] = (total + land_far[...].astype(f32)).astype(bf16)
    for copy in [far_copy, back] + first + passed + crossing + beside + onward + told + shared + away + near:
        copy.wait_send()


def local_tables():
    j = np.arange(KX * KY)
    angles = np.stack([j // KY, j % KY - KY // 2]) * (two_pi / BOX)
    return np.concatenate([np.cos(angles), np.sin(angles)]).astype(np.float32)


def column_block(pixel_count):
    lanes = pixel_count // 128
    return 128 * max(d for d in range(1, lanes + 1) if lanes % d == 0 and d <= 48)


def per_device_halves(group, particles, projections, ctf, defocus_group, offsets, routes):
    pix = KX * KY
    own = particles.shape[0]
    classes = projections.shape[0]
    n_groups = ctf.shape[0]
    n_orient, n_cls = lax.axis_size("orient"), lax.axis_size("cls")
    tables = jnp.asarray(local_tables())
    freq_across, freq_down = frequencies()
    group_onehot = (defocus_group[:, None] == jnp.arange(n_groups, dtype=jnp.int32)[None, :]).astype(bf16)
    ctf_rows = jnp.dot(group_onehot, ctf, preferred_element_type=f32)
    turns = jnp.mod(freq_across[None, :] * offsets[:, 0:1] + freq_down[None, :] * offsets[:, 1:2], BOX)
    angle = turns.astype(f32) * (two_pi / BOX)
    cos_base, sin_base = jnp.cos(angle), jnp.sin(angle)
    real_part = particles[:, :pix].astype(f32)
    imag_part = particles[:, pix:].astype(f32)
    first = (real_part * cos_base + imag_part * sin_base) * ctf_rows
    second = (imag_part * cos_base - real_part * sin_base) * ctf_rows
    aligned = jnp.concatenate([first, second], axis=0).astype(bf16)
    own_refs = projections.reshape(classes, 2, pix).transpose(1, 0, 2).reshape(2 * classes, pix)
    listed = jnp.any(routes.T[:, None, :] == jnp.arange(n_orient, dtype=jnp.int32)[None, :, None], axis=0)
    chosen = jnp.arange(n_groups, dtype=jnp.int32)[:, None] == defocus_group[None, :]
    meta = jnp.concatenate([listed, chosen], axis=0).astype(f32)
    meta = jnp.pad(meta, ((0, -meta.shape[0] % 8), (0, 128 - own)))
    block = column_block(pix)
    pieces = pix // block
    kd = 2 * n_cls * classes
    dma = pltpu.SemaphoreType.DMA
    vmem = pltpu.VMEM
    spec = pl.BlockSpec(memory_space=pltpu.VMEM)
    piece = own_refs.shape
    stack = (2, n_cls) + piece
    hops = group // 2 - 1
    out, evidence = pl.pallas_call(
        lambda *r: fused_kernel(group, n_cls, own, pieces, *r),
        out_shape=(jax.ShapeDtypeStruct(piece, bf16), jax.ShapeDtypeStruct((8, 128), f32)),
        in_specs=[spec] * 5,
        out_specs=(spec, spec),
        scratch_shapes=[
            vmem((group,) + aligned.shape, bf16),
            vmem(stack, bf16),
            vmem((group,) + meta.shape, f32),
            vmem((kd, block), f32),
            vmem((kd, block), f32),
            vmem((10 * kd, 128), f32),
            vmem((group, 8, 128), f32),
            vmem(stack, bf16),
            vmem((2, n_cls - 1) + piece, bf16),
            vmem(piece, bf16),
            vmem(piece, bf16),
        ]
        + [dma((pieces, hops))] * 2 + [dma((pieces,))] * 2 + [dma((pieces, hops))] * 2 + [dma((group - 1,))] * 2
        + [dma((n_cls - 1,))] * 4 + [dma((2,))] + [dma((group - 1,))] * 2
        + [dma((n_cls - 1,))] * 4 + [dma((2,)), dma((3,))],
        compiler_params=pltpu.CompilerParams(collective_id=0, has_side_effects=True, vmem_limit_bytes=VMEM_BYTES),
    )(aligned, own_refs, meta, ctf, tables)
    log_evidence = evidence[0, :own]
    data_sum = out.reshape(2, classes, pix).transpose(1, 0, 2).reshape(classes, 1, 2 * pix)
    return (log_evidence, data_sum)


def solution(mesh):
    placed = (
        P(("groups", "orient", "cls"), None),
        P("cls", "orient", None),
        P(),
        P(("groups", "orient", "cls")),
        P(("groups", "orient", "cls"), None),
        P(("groups", "orient", "cls"), None),
    )

    def per_device(particles, projections, *rest):
        group = mesh.shape["orient"] // 2
        held = 2 * particles.size * group
        fits = mesh.shape["orient"] == 2 * group and group > 2 and group % 2 == 0 and mesh.shape["cls"] > 1
        fits = fits and 4 * held <= VMEM_BYTES and 2 * group * particles.shape[0] <= 128
        fits = fits and projections.shape[1] == 1
        if fits:
            return per_device_halves(group, particles, projections, *rest)
        return per_device_slots(particles, projections, *rest)

    return jax.shard_map(
        per_device,
        mesh=mesh,
        in_specs=placed,
        out_specs=(P(("groups", "orient", "cls")), P(("groups", "cls"), "orient", None)),
        check_vma=False,
    )
```

```python
import functools
import math

import jax
import jax.numpy as jnp
import numpy as np
from jax import lax
from jax.experimental import pallas as pl
from jax.experimental.pallas import tpu as pltpu
from jax.sharding import PartitionSpec as P

KX = 86
KY = 192
BOX = 256


two_pi = 2.0 * math.pi
highest = lax.Precision.HIGHEST
local_across = np.array([0, 1, -1, 0, 0], dtype=np.int32)
local_down = np.array([0, 0, 0, 1, -1], dtype=np.int32)


def frequencies():
    column = jnp.arange(KX * KY, dtype=jnp.int32)
    return (column // KY, column % KY - KY // 2)


def rotation(shift_across, shift_down, freq_across, freq_down):
    turns = jnp.mod(freq_across * shift_across + freq_down * shift_down, BOX)
    angle = turns.astype(jnp.float32) * (two_pi / BOX)
    return (jnp.cos(angle), jnp.sin(angle))


def combine_stats(peaks, masses):
    top_value = jnp.max(peaks, axis=-1, keepdims=True)
    return top_value[..., 0] + jnp.log(jnp.sum(masses * jnp.exp(peaks - top_value), axis=-1))


def align_images(images, ctf_rows, shifts, freq_across, freq_down, pixel_count):
    real_part = images[:, :pixel_count].astype(jnp.float32)
    imag_part = images[:, pixel_count:].astype(jnp.float32)
    cos_base, sin_base = rotation(
        shifts[:, 0:1], shifts[:, 1:2], freq_across[None, :], freq_down[None, :]
    )
    first = (real_part * cos_base + imag_part * sin_base) * ctf_rows
    second = (imag_part * cos_base - real_part * sin_base) * ctf_rows
    return jnp.concatenate([first, second], axis=1).astype(jnp.bfloat16)


def spread_phase(table, ndim_rest):
    return table.reshape((table.shape[0],) + (1,) * ndim_rest + (table.shape[1],))


def turn_refs(ref_block, cos_shift, sin_shift, pixel_count):
    real_ref = ref_block[..., :pixel_count].astype(jnp.float32)
    imag_ref = ref_block[..., pixel_count:].astype(jnp.float32)
    cos_wide = spread_phase(cos_shift, real_ref.ndim - 1)
    sin_wide = spread_phase(sin_shift, real_ref.ndim - 1)
    first = real_ref[None] * cos_wide - imag_ref[None] * sin_wide
    second = real_ref[None] * sin_wide + imag_ref[None] * cos_wide
    turned = jnp.concatenate([first, second], axis=-1).astype(jnp.bfloat16)
    return (turned, real_ref * real_ref + imag_ref * imag_ref)


def back_rotate(summed, cos_shift, sin_shift, pixel_count):
    cos_wide = spread_phase(cos_shift, summed.ndim - 2)
    sin_wide = spread_phase(sin_shift, summed.ndim - 2)
    real_sum = summed[..., :pixel_count]
    imag_sum = summed[..., pixel_count:]
    first = jnp.sum(real_sum * cos_wide + imag_sum * sin_wide, axis=0)
    second = jnp.sum(imag_sum * cos_wide - real_sum * sin_wide, axis=0)
    return jnp.concatenate([first, second], axis=-1)


def slot_places(route_rows, orient_size):
    targets = route_rows.reshape(-1)
    onehot = (targets[:, None] == jnp.arange(orient_size, dtype=jnp.int32)[None, :]).astype(
        jnp.int32
    )
    place = jnp.arange(targets.shape[0], dtype=jnp.int32)
    earlier = (place[None, :] < place[:, None]).astype(jnp.float32)
    before = jnp.dot(earlier, onehot.astype(jnp.float32), precision=highest).astype(jnp.int32)
    return (targets, jnp.sum(before * onehot, axis=1))


def per_device_slots(particles, projections, ctf, defocus_group, offsets, routes):
    pixel_count = KX * KY
    own_count = particles.shape[0]
    route_count = routes.shape[1]
    class_local = projections.shape[0]
    directions = projections.shape[1]
    group_count = ctf.shape[0]
    orient_size = lax.axis_size("orient")
    capacity = max(2, (own_count * route_count + orient_size - 1) // orient_size)
    total_slots = orient_size * capacity
    freq_across, freq_down = frequencies()
    ctf_table = ctf.astype(jnp.float32)
    group_onehot = (
        defocus_group[:, None] == jnp.arange(group_count, dtype=jnp.int32)[None, :]
    ).astype(jnp.float32)
    ctf_rows = jnp.dot(group_onehot, ctf_table, precision=highest)
    aligned = align_images(particles, ctf_rows, offsets, freq_across, freq_down, pixel_count)
    targets, orders = slot_places(routes, orient_size)
    slot_ids = targets * capacity + orders
    matches = (slot_ids[None, :] == jnp.arange(total_slots, dtype=jnp.int32)[:, None]).astype(
        jnp.int32
    )
    picked = jnp.sum(matches.reshape(total_slots, own_count, route_count), axis=2)
    send_images = jnp.dot(picked.astype(jnp.bfloat16), aligned, preferred_element_type=jnp.float32)
    send_images = send_images.astype(jnp.bfloat16).reshape(orient_size, capacity, 2 * pixel_count)
    send_codes = jnp.sum(picked * (defocus_group + 1)[None, :], axis=1).reshape(
        orient_size, capacity
    )
    tiles, codes = (
        lax.all_to_all(send_images, "orient", split_axis=0, concat_axis=0, tiled=True),
        lax.all_to_all(send_codes, "orient", split_axis=0, concat_axis=0, tiled=True),
    )
    rows_in = tiles.reshape(total_slots, 2 * pixel_count)
    codes_in = codes.reshape(total_slots)
    slot_groups = (
        codes_in[:, None] - 1 == jnp.arange(group_count, dtype=jnp.int32)[None, :]
    ).astype(jnp.float32)
    occupied = codes_in > 0
    cos_shift, sin_shift = rotation(
        jnp.asarray(local_across, dtype=jnp.int32)[:, None],
        jnp.asarray(local_down, dtype=jnp.int32)[:, None],
        freq_across[None, :],
        freq_down[None, :],
    )
    shift_total = cos_shift.shape[0]
    ctf_square = ctf_table * ctf_table
    ref_piece = lax.all_gather(projections, "cls", axis=0, tiled=True)
    piece_rows = ref_piece.shape[0]
    group_size = 2
    grouped = ref_piece.reshape(piece_rows // group_size, group_size, directions, 2 * pixel_count)

    def one_group(ref_block):
        turned, magnitude = turn_refs(ref_block, cos_shift, sin_shift, pixel_count)
        products = lax.dot_general(
            rows_in,
            turned.reshape(-1, 2 * pixel_count),
            (((1,), (1,)), ((), ())),
            preferred_element_type=jnp.float32,
        )
        energy = lax.dot_general(
            ctf_square,
            magnitude.reshape(group_size * directions, pixel_count),
            (((1,), (1,)), ((), ())),
            precision=highest,
        )
        slot_energy = jnp.dot(slot_groups, energy, precision=highest).reshape(
            total_slots, 1, group_size, directions
        )
        return (
            products.reshape(total_slots, shift_total, group_size, directions) - 0.5 * slot_energy
        )

    stacked = lax.map(one_group, grouped)
    scores = jnp.transpose(stacked, (1, 2, 0, 3, 4)).reshape(
        total_slots, shift_total, piece_rows, directions
    )
    slot_peak = jnp.max(scores, axis=(1, 2, 3))
    slot_mass = jnp.sum(jnp.exp(scores - slot_peak[:, None, None, None]), axis=(1, 2, 3))
    back_peak, back_mass = (
        lax.all_to_all(
            slot_peak.reshape(orient_size, capacity),
            "orient",
            split_axis=0,
            concat_axis=0,
            tiled=True,
        ),
        lax.all_to_all(
            slot_mass.reshape(orient_size, capacity),
            "orient",
            split_axis=0,
            concat_axis=0,
            tiled=True,
        ),
    )
    match_table = matches.astype(jnp.float32)
    entry_peak = jnp.dot(back_peak.reshape(-1), match_table, precision=highest).reshape(
        own_count, route_count
    )
    entry_mass = jnp.dot(back_mass.reshape(-1), match_table, precision=highest).reshape(
        own_count, route_count
    )
    log_evidence = combine_stats(entry_peak, entry_mass)
    slot_value = jnp.dot(picked.astype(jnp.float32), log_evidence, precision=highest).reshape(
        orient_size, capacity
    )
    evidence_in = lax.all_to_all(
        slot_value, "orient", split_axis=0, concat_axis=0, tiled=True
    ).reshape(total_slots)
    live = occupied[:, None, None, None]
    exponent = jnp.where(live, scores - evidence_in[:, None, None, None], 0.0)
    weights = jnp.where(live, jnp.exp(exponent), 0.0).astype(jnp.bfloat16)
    class_group_size = 2

    def one_group(group_index):
        weight_part = lax.dynamic_slice_in_dim(
            weights, group_index * class_group_size, class_group_size, 2
        )
        summed = lax.dot_general(
            weight_part.reshape(total_slots, -1),
            rows_in,
            (((0,), (0,)), ((), ())),
            preferred_element_type=jnp.float32,
        )
        summed = summed.reshape(shift_total, class_group_size, directions, 2 * pixel_count)
        return back_rotate(summed, cos_shift, sin_shift, pixel_count)

    results = lax.map(
        one_group,
        jnp.arange(class_local * lax.axis_size("cls") // class_group_size, dtype=jnp.int32),
    )
    data_sum = lax.psum_scatter(
        results.reshape(class_local * lax.axis_size("cls"), directions, 2 * pixel_count).astype(
            jnp.bfloat16
        ),
        "cls",
        scatter_dimension=0,
        tiled=True,
    )
    return (log_evidence, data_sum)


MESH = pl.DeviceIdType.MESH
VMEM_BYTES = 48 * 2**20
f32 = jnp.float32
bf16 = jnp.bfloat16


def place_of(group):
    o, c = lax.axis_index("orient"), lax.axis_index("cls")
    return o // group, o % group, c


def greet(peers):
    barrier = pltpu.get_barrier_semaphore()
    for peer in peers:
        pl.semaphore_signal(barrier, inc=1, device_id=peer, device_id_type=MESH)
    pl.semaphore_wait(barrier, len(peers))


def remote(src, dst, send, recv, peer):
    return pltpu.make_async_remote_copy(
        src_ref=src, dst_ref=dst, send_sem=send, recv_sem=recv,
        device_id=peer, device_id_type=MESH,
    )


def turn_of(tables, turn, columns):
    axis = (turn - 1) // 2
    cos, sin = tables[axis : axis + 1, columns], tables[2 + axis : 3 + axis, columns]
    return cos, (sin if turn % 2 else -sin)


def fused_kernel(group, n_cls, own, pieces,
                 x_ref, phase_ref, chosen_ref, p_ref, m_ref, ctf_ref, tables,
                 sum_out, evidence_out,
                 ctf_rows, images, refs, metas, re, im, full, stats, sums, land, send_far, land_far,
                 x_send, x_recv, s_send, s_recv, f_send, f_recv, m_send, m_recv,
                 p_send, p_recv, q_send, q_recv, far_sem, e_send, e_recv,
                 near_send, near_recv, away_send, away_recv, back_sem, local):
    hi, m, c = place_of(group)
    pix = x_ref.shape[1] // 2
    width = pix // pieces
    classes = p_ref.shape[0] // 2
    n_groups = ctf_ref.shape[0]
    kd = 2 * n_cls * classes
    used = 2 * own * group
    sibling = m + 1 - 2 * (m % 2)
    at = lambda member: {"orient": hi * group + member, "cls": c}
    mates = [at((m + s) % group) for s in range(1, group)]
    hops = group // 2 - 1
    owners = [{"orient": hi * group + m, "cls": (c + s) % n_cls} for s in range(1, n_cls)]
    far = {"orient": (1 - hi) * group + m, "cls": c}
    greet(mates + owners + [far])

    far_copy = remote(p_ref, refs.at[hi, c], far_sem.at[0], far_sem.at[1], far)
    far_copy.start()
    kept = [
        pltpu.make_async_copy(p_ref, refs.at[hi, c], local.at[0]),
        pltpu.make_async_copy(m_ref, metas.at[m], local.at[1]),
    ]
    first = [remote(p_ref, refs.at[hi, c], p_send.at[s], p_recv.at[s], peer) for s, peer in enumerate(owners)]
    cols = [pl.ds(q * width, width) for q in range(pieces)]
    crossing, beside, onward = [], [], []
    for q in range(pieces):
        for k in range(hops):
            crossing.append(remote(images.at[m, :, cols[q]], images.at[m, :, cols[q]], x_send.at[q, k], x_recv.at[q, k],
                                   at((m + 2 * (k + 1)) % group)))
            slot = images.at[(m + group - 2 * (k + 1)) % group, :, cols[q]]
            onward.append(remote(slot, slot, f_send.at[q, k], f_recv.at[q, k], at(sibling)))
        beside.append(remote(images.at[m, :, cols[q]], images.at[m, :, cols[q]], s_send.at[q], s_recv.at[q], at(sibling)))
    told = [remote(m_ref, metas.at[m], m_send.at[s], m_recv.at[s], peer) for s, peer in enumerate(mates)]
    for copy in first + told + kept:
        copy.start()

    period = phase_ref.shape[1] - 1
    step_cos, step_sin = phase_ref[0, period], phase_ref[1, period]
    blocks = width // 128

    def align_block(phases, q, offset):
        cos, sin = phases[0]
        there = pl.ds(pl.multiple_of(q * width + offset, 128), 128)
        mirror = pl.ds(pl.multiple_of(pix + q * width + offset, 128), 128)
        real, imag = x_ref[:, there].astype(f32), x_ref[:, mirror].astype(f32)
        scale = ctf_rows[:, pl.ds(pl.multiple_of(offset, 128), 128)]
        both = [(real * cos + imag * sin) * scale, (imag * cos - real * sin) * scale]
        images[m, :, there] = jnp.concatenate(both, axis=0).astype(bf16)
        ahead = (cos * step_cos - sin * step_sin, sin * step_cos + cos * step_sin)
        return phases[1:] + [ahead]

    def align_some(i, phases, q):
        for u in range(period):
            phases = align_block(phases, q, (i * period + u) * 128)
        return phases

    phases = [(phase_ref[0, u], phase_ref[1, u]) for u in range(period)]
    for q in range(pieces):
        ctf_rows[...] = jnp.dot(chosen_ref[...], ctf_ref[:, q * width : (q + 1) * width], preferred_element_type=f32)
        phases = lax.fori_loop(0, blocks // period, functools.partial(align_some, q=q), phases)
        for u in range(blocks % period):
            phases = align_block(phases, q, (blocks // period * period + u) * 128)
        for copy in crossing[q * hops : (q + 1) * hops] + [beside[q]]:
            copy.start()
    far_copy.wait_recv()
    there = refs.at[1 - hi, c]
    passed = [remote(there, there, q_send.at[s], q_recv.at[s], peer) for s, peer in enumerate(owners)]
    for copy in passed:
        copy.start()
    full[...] = jnp.zeros_like(full)
    for copy in kept:
        copy.wait()
    for copy in first + passed:
        copy.wait_recv()

    def all_images(q):
        return jnp.concatenate([images[s, :, q * width : (q + 1) * width] for s in range(group)], axis=0)

    def score_piece(q):
        here = slice(q * width, (q + 1) * width)
        for h in range(2):
            for k in range(n_cls):
                row = (h * n_cls + k) * classes
                block = refs[h, k, :, here].astype(f32)
                re[row : row + classes] = block[:classes]
                im[row : row + classes] = block[classes:]
        p, q_ = re[...], im[...]
        square = ctf_ref[:, here].astype(f32)
        energy = lax.dot_general(p * p + q_ * q_, square * square, (((1,), (1,)), ((), ())),
                                 precision=highest, preferred_element_type=f32)
        rows = [p.astype(bf16), q_.astype(bf16)]
        for turn in range(1, 5):
            cos, sin = turn_of(tables, turn, here)
            rows += [(p * cos - q_ * sin).astype(bf16), (p * sin + q_ * cos).astype(bf16)]
        turned = jnp.concatenate(rows, axis=0)
        for copy in onward[q * hops : (q + 1) * hops] + [beside[q]]:
            copy.wait_recv()
        full[:, :used] += lax.dot_general(turned, all_images(q), (((1,), (1,)), ((), ())), preferred_element_type=f32)
        return energy

    energy = jnp.zeros((kd, n_groups), f32)
    for q in range(pieces):
        for copy, pass_on in zip(crossing[q * hops : (q + 1) * hops], onward[q * hops : (q + 1) * hops]):
            copy.wait_recv()
            pass_on.start()
        if q:
            energy += score_piece(q - 1)
    energy += score_piece(pieces - 1)
    for copy in told:
        copy.wait_recv()

    lanes = full.shape[1]
    meta = metas[0]
    for s in range(1, group):
        meta += pltpu.roll(metas[s], 2 * own * s, 1)
    n_orient = 2 * group
    listed, onehot = meta[:n_orient], meta[n_orient : n_orient + n_groups]
    level = jnp.dot(energy, onehot, precision=highest, preferred_element_type=f32)
    row_of = lax.broadcasted_iota(jnp.int32, listed.shape, 0)
    mine = [jnp.sum(jnp.where(row_of == h * group + m, listed, 0.0), axis=0, keepdims=True) for h in range(2)]
    live = jnp.concatenate([jnp.broadcast_to(row, (kd // 2, lanes)) for row in mine], axis=0) > 0
    score = []
    for turn in range(5):
        real, imag = full[2 * kd * turn : 2 * kd * turn + kd], full[2 * kd * turn + kd : 2 * kd * (turn + 1)]
        score.append(real + pltpu.roll(imag, lanes - own, 1) - 0.5 * level)
    low = -3.0e38
    peak = functools.reduce(jnp.maximum, score)
    peak = jnp.max(jnp.where(live, peak, low), axis=0, keepdims=True)
    mass = sum(jnp.where(live, jnp.exp(jnp.where(live, v - peak, 0.0)), 0.0) for v in score)
    mass = jnp.sum(mass, axis=0, keepdims=True)
    half_row = lax.broadcasted_iota(jnp.int32, (8, lanes), 0)
    stats[m] = jnp.where(half_row == 0, peak, jnp.where(half_row == 1, mass, 0.0))
    shared = [remote(stats.at[m], stats.at[m], e_send.at[s], e_recv.at[s], peer) for s, peer in enumerate(mates)]
    for copy in shared:
        copy.start()
    for copy in shared:
        copy.wait_recv()
    held = [stats[s] for s in range(group)]
    top = functools.reduce(jnp.maximum, [v[0:1] for v in held])
    evidence = top + jnp.log(sum(v[1:2] * jnp.exp(v[0:1] - top) for v in held))
    result = jnp.zeros((8, lanes), f32)
    wide = jnp.broadcast_to(evidence, (8, lanes))
    for s in range(group):
        moved = pltpu.roll(wide, lanes - 2 * own * s, 1) if s else wide
        result = jnp.where(m == s, moved, result)
    evidence_out[...] = result
    weights = []
    for value in score:
        weight = jnp.where(live, jnp.exp(jnp.where(live, value - evidence, 0.0)), 0.0)
        weights += [weight.astype(bf16), pltpu.roll(weight, own, 1).astype(bf16)]
    weights = jnp.concatenate(weights, axis=0)[:, :used]

    away, near = [], []
    for s in range(1, n_cls):
        to = (c + s) % n_cls
        away.append(remote(sums.at[1 - hi, to], land.at[1, s - 1], away_send.at[s - 1], away_recv.at[s - 1], owners[s - 1]))
        near.append(remote(sums.at[hi, to], land.at[0, s - 1], near_send.at[s - 1], near_recv.at[s - 1], owners[s - 1]))
    for q in range(pieces):
        here = slice(q * width, (q + 1) * width)
        summed = jnp.dot(weights, all_images(q), preferred_element_type=f32)
        real_sum, imag_sum = summed[:kd], summed[kd : 2 * kd]
        for turn in range(1, 5):
            cos, sin = turn_of(tables, turn, here)
            real, imag = summed[2 * kd * turn : 2 * kd * turn + kd], summed[2 * kd * turn + kd : 2 * kd * (turn + 1)]
            real_sum += real * cos + imag * sin
            imag_sum += imag * cos - real * sin
        for h in range(2):
            for k in range(n_cls):
                row = (h * n_cls + k) * classes
                sums[h, k, :classes, here] = real_sum[row : row + classes].astype(bf16)
                sums[h, k, classes:, here] = imag_sum[row : row + classes].astype(bf16)
    for copy in away + near:
        copy.start()
    for copy in away:
        copy.wait_recv()
    total = sums[1 - hi, c].astype(f32)
    for s in range(n_cls - 1):
        total += land[1, s].astype(f32)
    send_far[...] = total.astype(bf16)
    back = remote(send_far, land_far, back_sem.at[0], back_sem.at[1], far)
    back.start()
    for copy in near:
        copy.wait_recv()
    total = sums[hi, c].astype(f32)
    for s in range(n_cls - 1):
        total += land[0, s].astype(f32)
    back.wait_recv()
    sum_out[...] = (total + land_far[...].astype(f32)).astype(bf16)
    for copy in [far_copy, back] + first + passed + crossing + beside + onward + told + shared + away + near:
        copy.wait_send()


def local_tables():
    j = np.arange(KX * KY)
    angles = np.stack([j // KY, j % KY - KY // 2]) * (two_pi / BOX)
    return np.concatenate([np.cos(angles), np.sin(angles)]).astype(np.float32)


def column_block(pixel_count):
    lanes = pixel_count // 128
    return 128 * max(d for d in range(1, lanes + 1) if lanes % d == 0 and d <= 48)


def per_device_halves(group, particles, projections, ctf, defocus_group, offsets, routes):
    pix = KX * KY
    own = particles.shape[0]
    classes = projections.shape[0]
    n_groups = ctf.shape[0]
    n_orient, n_cls = lax.axis_size("orient"), lax.axis_size("cls")
    tables = jnp.asarray(local_tables())
    group_onehot = (defocus_group[:, None] == jnp.arange(n_groups, dtype=jnp.int32)[None, :]).astype(bf16)
    span = math.lcm(128, KY)
    column = jnp.arange(span, dtype=jnp.int32)
    across = jnp.concatenate([column // KY, jnp.full((128,), span // KY, jnp.int32)])
    down = jnp.concatenate([column % KY - KY // 2, jnp.zeros((128,), jnp.int32)])
    across, down = across.reshape(-1, 1, 128), down.reshape(-1, 1, 128)
    phases = jnp.stack(rotation(offsets[None, :, 0:1], offsets[None, :, 1:2], across, down))
    own_refs = projections.reshape(classes, 2, pix).transpose(1, 0, 2).reshape(2 * classes, pix)
    listed = jnp.any(routes.T[:, None, :] == jnp.arange(n_orient, dtype=jnp.int32)[None, :, None], axis=0)
    chosen = jnp.arange(n_groups, dtype=jnp.int32)[:, None] == defocus_group[None, :]
    meta = jnp.concatenate([listed, chosen], axis=0).astype(f32)
    meta = jnp.pad(meta, ((0, -meta.shape[0] % 8), (0, 128 - own)))
    block = column_block(pix)
    pieces = pix // block
    kd = 2 * n_cls * classes
    dma = pltpu.SemaphoreType.DMA
    vmem = pltpu.VMEM
    spec = pl.BlockSpec(memory_space=pltpu.VMEM)
    piece = own_refs.shape
    stack = (2, n_cls) + piece
    hops = group // 2 - 1
    out, evidence = pl.pallas_call(
        lambda *r: fused_kernel(group, n_cls, own, pieces, *r),
        out_shape=(jax.ShapeDtypeStruct(piece, bf16), jax.ShapeDtypeStruct((8, 128), f32)),
        in_specs=[spec] * 7,
        out_specs=(spec, spec),
        scratch_shapes=[
            vmem((own, block), f32),
            vmem((group, 2 * own, pix), bf16),
            vmem(stack, bf16),
            vmem((group,) + meta.shape, f32),
            vmem((kd, block), f32),
            vmem((kd, block), f32),
            vmem((10 * kd, 128), f32),
            vmem((group, 8, 128), f32),
            vmem(stack, bf16),
            vmem((2, n_cls - 1) + piece, bf16),
            vmem(piece, bf16),
            vmem(piece, bf16),
        ]
        + [dma((pieces, hops))] * 2 + [dma((pieces,))] * 2 + [dma((pieces, hops))] * 2 + [dma((group - 1,))] * 2
        + [dma((n_cls - 1,))] * 4 + [dma((2,))] + [dma((group - 1,))] * 2
        + [dma((n_cls - 1,))] * 4 + [dma((2,)), dma((2,))],
        compiler_params=pltpu.CompilerParams(collective_id=0, has_side_effects=True, vmem_limit_bytes=VMEM_BYTES),
    )(particles, phases, group_onehot, own_refs, meta, ctf, tables)
    log_evidence = evidence[0, :own]
    data_sum = out.reshape(2, classes, pix).transpose(1, 0, 2).reshape(classes, 1, 2 * pix)
    return (log_evidence, data_sum)


def solution(mesh):
    placed = (
        P(("groups", "orient", "cls"), None),
        P("cls", "orient", None),
        P(),
        P(("groups", "orient", "cls")),
        P(("groups", "orient", "cls"), None),
        P(("groups", "orient", "cls"), None),
    )

    def per_device(particles, projections, *rest):
        group = mesh.shape["orient"] // 2
        held = 2 * particles.size * group
        fits = mesh.shape["orient"] == 2 * group and group > 2 and group % 2 == 0 and mesh.shape["cls"] > 1
        fits = fits and 4 * held <= VMEM_BYTES and 2 * group * particles.shape[0] <= 128
        fits = fits and projections.shape[1] == 1
        if fits:
            return per_device_halves(group, particles, projections, *rest)
        return per_device_slots(particles, projections, *rest)

    return jax.shard_map(
        per_device,
        mesh=mesh,
        in_specs=placed,
        out_specs=(P(("groups", "orient", "cls")), P(("groups", "cls"), "orient", None)),
        check_vma=False,
    )
```
